32 devices in a mesh: expert: 16 (over z, y, core), dp: 2 (over x).
Axes of the slice: x: 2, y: 2, z: 4, core: 2. Of those that a mesh axis runs over, the one named last changes fastest.
Arguments:
- tokens: bfloat16 [4096, 2048], P(('expert', 'dp')), may hold values from -6 to 6
- targets: bfloat16 [4096, 2048], P(('expert', 'dp')), may hold values from -6 to 6
- router: bfloat16 [2048, 16], replicated, may hold values from -0.125 to 0.125
- picks: int32 [4096, 16, 4], P(('expert', 'dp')), may hold values from 0 to 1, as said below
- w_gate_up: bfloat16 [16, 2, 1408, 2048], P('expert', None, 'dp'), may hold values from -0.125 to 0.125
- w_down: bfloat16 [16, 1408, 2048], P('expert', 'dp'), may hold values from -0.15625 to 0.15625
- v_gate_up: bfloat16 [16, 2, 1408, 2048], P('expert', None, 'dp'), may hold values from -0.125 to 0.125
- v_down: bfloat16 [16, 1408, 2048], P('expert', 'dp'), may hold values from -0.15625 to 0.15625
Outputs:
- mixed: bfloat16 [4096, 2048], P(('expert', 'dp'))
- hvp_gate_up: float32 [16, 2, 1408, 2048], P('expert', None, 'dp')
- hvp_down: float32 [16, 1408, 2048], P('expert', 'dp')
The draws below stay inside these ranges and needn't reach their ends.
Inputs may be any that keep to these rules, and one draw needn't show every extreme that they name: In every block of 128 tokens (one device's rows), for each expert e and slot c exactly one token t has picks[t, e, c] = 1, and an expert never picks a token twice.
All inputs are finite; a program needn't handle non-finite values.
Results may differ from the reference program's by a relative error of at most 0.009.
Values may be sent and summed in bfloat16 or wider, within the bound.
A program may use at most 128 MiB of HBM per device.

```python
import math
import jax
import jax.numpy as jnp
from jax import lax

D = 2048
FF = 1408
TOK_DEV = 128
CAP = 4
EXPERTS = 16
TOKENS = 4096


def draw_picks(key, part):
    blocks = TOKENS // TOK_DEV
    raw = jax.random.randint(key, (blocks, EXPERTS, TOK_DEV), 0, 1 << 20)
    scores = raw * TOK_DEV + jnp.arange(TOK_DEV, dtype=jnp.int32)
    order = jnp.argsort(scores, axis=-1)
    chosen = order[:, :, :CAP]
    hits = (jnp.arange(TOK_DEV, dtype=jnp.int32)[None, :, None, None] == chosen[:, None, :, :]).astype(jnp.int32)
    return hits.reshape(TOKENS, EXPERTS, CAP)


def level_of(rng, dims, cuts, low, top_value):
    level = 1.0
    for axis_at, shards_of in cuts:
        draws = jax.random.uniform(jax.random.fold_in(jax.random.fold_in(rng, 6), axis_at), (shards_of,), jnp.float32, low / len(cuts), top_value / len(cuts))
        level = level * jnp.repeat(jnp.exp(draws), dims[axis_at] // shards_of).reshape((-1,) + (1,) * (len(dims) - 1 - axis_at))
    return level


def normal_values(own_key, shape, deviation, reach, cuts=(), kind=jnp.bfloat16):
    factor_of = level_of(own_key, shape, cuts, -0.22, 0.18) if cuts else 1.0
    array = jax.random.normal(own_key, shape, jnp.float32) * deviation * factor_of
    return jnp.minimum(jnp.maximum(array, -reach), reach).astype(kind)


def setup_inputs(seed: int = 0) -> dict:
    key_list = jax.random.split(jax.random.key(seed), 9)
    tokens = normal_values(key_list[0], (TOKENS, D), 1.0, 6.0, ((0, 32),))
    targets = normal_values(key_list[1], (TOKENS, D), 1.0, 6.0, ((0, 32),))
    router = normal_values(key_list[2], (D, EXPERTS), D ** -0.5, 0.125)
    picks = draw_picks(jax.random.fold_in(key_list[8], 71), 0)
    w_gate_up = normal_values(key_list[4], (EXPERTS, 2, FF, D), D ** -0.5, 0.125, ((0, 16), (2, 2)))
    w_down = normal_values(key_list[5], (EXPERTS, FF, D), FF ** -0.5, 0.15625, ((0, 16), (1, 2)))
    v_gate_up = normal_values(key_list[6], (EXPERTS, 2, FF, D), D ** -0.5, 0.125, ((0, 16), (2, 2)))
    v_down = normal_values(key_list[7], (EXPERTS, FF, D), FF ** -0.5, 0.15625, ((0, 16), (1, 2)))
    return dict(tokens=tokens, targets=targets, router=router, picks=picks, w_gate_up=w_gate_up, w_down=w_down, v_gate_up=v_gate_up, v_down=v_down)


def forward_pieces(rows, wgu, vgu):
    gate_pre = jnp.dot(rows, wgu[0].T, preferred_element_type=jnp.float32)
    up_pre = jnp.dot(rows, wgu[1].T, preferred_element_type=jnp.float32)
    gate_dot = jnp.dot(rows, vgu[0].T, preferred_element_type=jnp.float32)
    up_dot = jnp.dot(rows, vgu[1].T, preferred_element_type=jnp.float32)
    sigma = jax.nn.sigmoid(gate_pre)
    active = gate_pre * sigma
    slope = sigma * (1.0 + gate_pre * (1.0 - sigma))
    curve = sigma * (1.0 - sigma) * (2.0 + gate_pre * (1.0 - 2.0 * sigma))
    act_dot = slope * gate_dot
    hidden = (active * up_pre).astype(jnp.bfloat16)
    hidden_dot = (act_dot * up_pre + active * up_dot).astype(jnp.bfloat16)
    return (up_pre, gate_dot, up_dot, active, slope, curve, act_dot, hidden, hidden_dot)

def reference(tokens, targets, router, picks, w_gate_up, w_down, v_gate_up, v_down):
    blocks = TOKENS // TOK_DEV
    gates = jax.nn.sigmoid(jnp.dot(tokens, router, preferred_element_type=jnp.float32))
    offsets = jnp.arange(TOK_DEV, dtype=jnp.int32)
    where = lax.optimization_barrier(jnp.sum(picks.reshape(blocks, TOK_DEV, EXPERTS, CAP) * offsets[None, :, None, None], axis=1))
    index = where + (jnp.arange(blocks, dtype=jnp.int32) * TOK_DEV)[:, None, None]
    index = jnp.transpose(index, (1, 0, 2)).reshape(EXPERTS, blocks * CAP).astype(jnp.int32)
    picked = jnp.take_along_axis(gates.T, index, axis=1)
    scale = 1.0 / math.sqrt(blocks * CAP)

    def forward(item):
        wgu, wdown, vgu, vdown, rows_index = item
        rows = tokens[rows_index]
        pieces = forward_pieces(rows, wgu, vgu)
        hidden, hidden_dot = (pieces[7], pieces[8])
        result = jnp.dot(hidden, wdown, preferred_element_type=jnp.float32)
        result_dot = jnp.dot(hidden_dot, wdown, preferred_element_type=jnp.float32) + jnp.dot(hidden, vdown, preferred_element_type=jnp.float32)
        return (result.astype(jnp.bfloat16), result_dot.astype(jnp.bfloat16))
    outs, outs_dot = lax.map(forward, (w_gate_up, w_down, v_gate_up, v_down, index))
    flat = index.reshape(-1)
    weight = picked.reshape(-1, 1)
    combined = jnp.zeros((TOKENS, D), jnp.float32).at[flat].add(weight * outs.reshape(-1, D).astype(jnp.float32))
    combined_dot = jnp.zeros((TOKENS, D), jnp.float32).at[flat].add(weight * outs_dot.reshape(-1, D).astype(jnp.float32))
    mixed = combined.astype(jnp.bfloat16)
    resid = scale * (combined - targets.astype(jnp.float32))
    resid_dot = scale * combined_dot

    def backward(item):
        wgu, wdown, vgu, vdown, rows_index, gate_col = item
        rows = tokens[rows_index]
        up_pre, gate_dot, up_dot, active, slope, curve, act_dot, hidden, hidden_dot = forward_pieces(rows, wgu, vgu)
        cot = (gate_col[:, None] * resid[rows_index]).astype(jnp.bfloat16)
        cot_dot = (gate_col[:, None] * resid_dot[rows_index]).astype(jnp.bfloat16)
        grad_hid = jnp.dot(cot, wdown.T, preferred_element_type=jnp.float32)
        grad_hdot = jnp.dot(cot_dot, wdown.T, preferred_element_type=jnp.float32) + jnp.dot(cot, vdown.T, preferred_element_type=jnp.float32)
        down_term = jnp.dot(hidden_dot.T, cot, preferred_element_type=jnp.float32) + jnp.dot(hidden.T, cot_dot, preferred_element_type=jnp.float32)
        gate_term = ((grad_hdot * up_pre + grad_hid * up_dot) * slope + grad_hid * up_pre * curve * gate_dot).astype(jnp.bfloat16)
        up_term = (grad_hdot * active + grad_hid * act_dot).astype(jnp.bfloat16)
        hvp_gate = jnp.dot(gate_term.T, rows, preferred_element_type=jnp.float32)
        hvp_up = jnp.dot(up_term.T, rows, preferred_element_type=jnp.float32)
        return (jnp.stack([hvp_gate, hvp_up]), down_term)
    hvp_gate_up, hvp_down = lax.map(backward, (w_gate_up, w_down, v_gate_up, v_down, index, picked))
    return (mixed, hvp_gate_up, hvp_down)
```

```python
import functools
import math

import jax
import jax.numpy as jnp
from jax import lax
from jax.experimental import pallas as pl
from jax.experimental.pallas import tpu as pltpu
from jax.sharding import PartitionSpec as P


def regroup(block, lead):
    count, total, width = block.shape
    parted = block.reshape(count, lead, total // lead, width)
    return jnp.swapaxes(parted, 0, 1).reshape(lead, count * total // lead, width)


def local(tokens, targets, router, picks, w_gate_up, w_down, v_gate_up, v_down):
    highest = lax.Precision.HIGHEST
    n_exp = lax.axis_size("expert")
    exp_dev = w_down.shape[0]
    onehot = picks.astype(jnp.bfloat16)
    gates = jax.nn.sigmoid(jnp.dot(tokens, router, preferred_element_type=jnp.float32))
    outgoing = jnp.einsum("tec,td->ecd", onehot, tokens, preferred_element_type=jnp.float32).astype(
        jnp.bfloat16
    )
    arrived = lax.all_to_all(outgoing, "expert", split_axis=0, concat_axis=0, tiled=True)
    rows = lax.all_gather(regroup(arrived, exp_dev), "dp", axis=1, tiled=True)
    scale = 1.0 / math.sqrt(rows.shape[1])
    primal = jnp.einsum("ekfd,erd->ekfr", w_gate_up, rows, preferred_element_type=jnp.float32)
    tangent = jnp.einsum("ekfd,erd->ekfr", v_gate_up, rows, preferred_element_type=jnp.float32)
    gate_pre, up_pre = (primal[:, 0], primal[:, 1])
    gate_dot, up_dot = (tangent[:, 0], tangent[:, 1])
    sigma = jax.nn.sigmoid(gate_pre)
    active = gate_pre * sigma
    slope = sigma * (1.0 + gate_pre * (1.0 - sigma))
    curve = sigma * (1.0 - sigma) * (2.0 + gate_pre * (1.0 - 2.0 * sigma))
    act_dot = slope * gate_dot
    hidden = (active * up_pre).astype(jnp.bfloat16)
    hidden_dot = (act_dot * up_pre + active * up_dot).astype(jnp.bfloat16)
    part_out = jnp.einsum("efr,efd->erd", hidden, w_down, preferred_element_type=jnp.float32)
    part_dot = jnp.einsum(
        "efr,efd->erd", hidden_dot, w_down, preferred_element_type=jnp.float32
    ) + jnp.einsum("efr,efd->erd", hidden, v_down, preferred_element_type=jnp.float32)
    own_out, own_dot = (
        lax.psum_scatter(part_out, "dp", scatter_dimension=1, tiled=True),
        lax.psum_scatter(part_dot, "dp", scatter_dimension=1, tiled=True),
    )
    back_out = regroup(own_out.astype(jnp.bfloat16), n_exp)
    back_dot = regroup(own_dot.astype(jnp.bfloat16), n_exp)
    ret_out, ret_dot = (
        lax.all_to_all(back_out, "expert", split_axis=0, concat_axis=0, tiled=True),
        lax.all_to_all(back_dot, "expert", split_axis=0, concat_axis=0, tiled=True),
    )
    ret_out = ret_out.astype(jnp.float32)
    ret_dot = ret_dot.astype(jnp.float32)
    weighted = picks.astype(jnp.float32) * gates[:, :, None]
    combined = jnp.einsum("tec,ecd->td", weighted, ret_out, precision=highest)
    combined_dot = jnp.einsum("tec,ecd->td", weighted, ret_dot, precision=highest)
    mixed = combined.astype(jnp.bfloat16)
    resid = scale * (combined - targets.astype(jnp.float32))
    resid_dot = scale * combined_dot
    cot_send = jnp.einsum("tec,td->ecd", weighted, resid, precision=highest).astype(jnp.bfloat16)
    cdot_send = jnp.einsum("tec,td->ecd", weighted, resid_dot, precision=highest).astype(
        jnp.bfloat16
    )
    cot_got, cdot_got = (
        lax.all_to_all(cot_send, "expert", split_axis=0, concat_axis=0, tiled=True),
        lax.all_to_all(cdot_send, "expert", split_axis=0, concat_axis=0, tiled=True),
    )
    own_cot = regroup(cot_got, exp_dev)
    own_cdot = regroup(cdot_got, exp_dev)
    cot_rows, cdot_rows = (
        lax.all_gather(own_cot, "dp", axis=1, tiled=True),
        lax.all_gather(own_cdot, "dp", axis=1, tiled=True),
    )
    grad_hid = jnp.einsum("erd,efd->efr", cot_rows, w_down, preferred_element_type=jnp.float32)
    grad_hdot = jnp.einsum(
        "erd,efd->efr", cdot_rows, w_down, preferred_element_type=jnp.float32
    ) + jnp.einsum("erd,efd->efr", cot_rows, v_down, preferred_element_type=jnp.float32)
    hvp_down = jnp.einsum(
        "efr,erd->efd", hidden_dot, cot_rows, preferred_element_type=jnp.float32
    ) + jnp.einsum("efr,erd->efd", hidden, cdot_rows, preferred_element_type=jnp.float32)
    gate_term = (
        (grad_hdot * up_pre + grad_hid * up_dot) * slope + grad_hid * up_pre * curve * gate_dot
    ).astype(jnp.bfloat16)
    up_term = (grad_hdot * active + grad_hid * act_dot).astype(jnp.bfloat16)
    both_terms = jnp.stack([gate_term, up_term], axis=1)
    hvp_gate_up = jnp.einsum("ekfr,erd->ekfd", both_terms, rows, preferred_element_type=jnp.float32)
    return (mixed, hvp_gate_up, hvp_down)


f32, bf16 = jnp.float32, jnp.bfloat16
NT = (((1,), (1,)), ((), ()))
TN = (((0,), (0,)), ((), ()))
PIECES = 4


def mm(a, b, dims=(((1,), (0,)), ((), ()))):
    return lax.dot_general(a, b, dims, preferred_element_type=f32)


def iota2(shape, dim):
    return lax.broadcasted_iota(jnp.int32, shape, dim)


def main_kernel(
    n_exp, ff, width,
    tok, tgt, router, onehot, wgu_hbm, wd_hbm, vgu_hbm, vd_hbm,
    mixed, rows, hh, cc, terms,
    wgu, vgu, wd, vd,
    send, recv, ret_send, ret_recv, xsend, xrecv, own, hht, keep, gstack, btk, gcol,
    wsem, ssem, rsem, fs_sem, fr_sem, xs_sem, xr_sem,
):
    me = lax.axis_index("expert")
    peer = 1 - lax.axis_index("dp")
    piece = width // PIECES
    half = n_exp * 4
    blocks = n_exp * 16
    scale = 1.0 / math.sqrt(2 * half)

    loads = [
        pltpu.make_async_copy(src, dst, wsem.at[i])
        for i, (src, dst) in enumerate(
            [(wgu_hbm, wgu), (vgu_hbm, vgu), (wd_hbm, wd), (vd_hbm, vd)]
        )
    ]
    for load in loads:
        load.start()

    barrier = pltpu.get_barrier_semaphore()

    @pl.loop(1, n_exp)
    def _(k):
        pl.semaphore_signal(
            barrier, inc=1, device_id={"expert": lax.rem(me + k, n_exp)},
            device_id_type=pl.DeviceIdType.MESH,
        )

    pl.semaphore_signal(barrier, inc=1, device_id={"dp": peer}, device_id_type=pl.DeviceIdType.MESH)

    def hop(t, k, src, dst):
        to = lax.rem(me + k, n_exp)
        return pltpu.make_async_remote_copy(
            src_ref=src.at[to], dst_ref=dst.at[me], send_sem=ssem.at[t, k], recv_sem=rsem.at[t, k],
            device_id={"expert": to}, device_id_type=pl.DeviceIdType.MESH,
        )

    def arrival(t, k, src, dst):
        come = lax.rem(me + n_exp - k, n_exp)
        return pltpu.make_async_remote_copy(
            src_ref=src.at[come], dst_ref=dst.at[come], send_sem=ssem.at[t, k],
            recv_sem=rsem.at[t, k], device_id={"expert": come}, device_id_type=pl.DeviceIdType.MESH,
        )

    def relay(t, k, buf):
        come = lax.rem(me + n_exp - k, n_exp)
        return pltpu.make_async_remote_copy(
            src_ref=buf.at[0, come], dst_ref=buf.at[1, come], send_sem=fs_sem.at[t, k],
            recv_sem=fr_sem.at[t, k], device_id={"dp": peer}, device_id_type=pl.DeviceIdType.MESH,
        )

    def cross(t, p):
        return pltpu.make_async_remote_copy(
            src_ref=xsend.at[t, p], dst_ref=xrecv.at[t, p], send_sem=xs_sem.at[t, p],
            recv_sem=xr_sem.at[t, p], device_id={"dp": peer}, device_id_type=pl.DeviceIdType.MESH,
        )

    def spread(t, src, dst):
        @pl.loop(1, n_exp)
        def _(k):
            hop(t, k, src, dst).start()

        dst[me] = src[me]

    row_b, col_b = iota2((blocks, half), 0), iota2((blocks, half), 1)
    all_pieces = jnp.where(
        ((row_b >> 4) == (col_b >> 2)) & ((row_b & 3) == (col_b & 3)), 1.0, 0.0
    ).astype(bf16)
    picked_t = mm(all_pieces, onehot[...], NT)
    row_t = iota2(picked_t.shape, 0)
    for p in range(PIECES):
        btk[:, p * 128 : (p + 1) * 128] = jnp.where(
            ((row_t >> 2) & 3) == p, picked_t, 0.0
        ).astype(bf16)
    stacked = jnp.concatenate([tok[:, p * piece : (p + 1) * piece] for p in range(PIECES)], axis=0)
    send[0] = mm(btk[...], stacked).astype(bf16).reshape(n_exp, 16, piece)
    pl.semaphore_wait(barrier, n_exp)
    spread(0, send.at[0], recv.at[0, 0])
    relay(0, 0, recv.at[0]).start()

    gates = jax.nn.sigmoid(mm(tok[...], router[...]))
    g_hi = gates.astype(bf16)
    g_lo = (gates - g_hi.astype(f32)).astype(bf16)
    lane_e, col_e = iota2((n_exp, blocks), 0), iota2((n_exp, blocks), 1)
    widen = jnp.where(lane_e == (col_e >> 4), 1.0, 0.0).astype(bf16)
    weight = mm(onehot[...], all_pieces, NT) * (mm(g_hi, widen) + mm(g_lo, widen))
    w_hi = weight.astype(bf16).astype(f32)
    w_lo = weight - w_hi
    col_w = iota2(weight.shape, 1)
    for p in range(PIECES):
        at_piece = ((col_w >> 2) & 3) == p
        gstack[p * 256 : p * 256 + 128] = jnp.where(at_piece, w_hi, 0.0).astype(bf16)
        gstack[p * 256 + 128 : p * 256 + 256] = jnp.where(at_piece, w_lo, 0.0).astype(bf16)
    by_expert = mm(picked_t.astype(bf16), g_hi) + mm(picked_t.astype(bf16), g_lo)
    own_lane = (iota2(by_expert.shape, 0) >> 4) == iota2(by_expert.shape, 1)
    gcol[...] = jnp.broadcast_to(
        jnp.sum(jnp.where(own_lane, by_expert, 0.0), axis=1, keepdims=True), gcol.shape
    )


    def to_rows_matrix():
        rr, cp = iota2((blocks, blocks), 0), iota2((blocks, blocks), 1)
        inside = lax.rem(rr, half)
        want = (inside >> 2) * 16 + lax.div(rr, half) * 4 + (inside & 3)
        return jnp.where(cp == want, 1.0, 0.0).astype(bf16)

    perm = to_rows_matrix()

    def unpack(buf, dst, row0):
        flat = mm(perm, buf[...].reshape(blocks, piece)).astype(bf16)
        for p in range(PIECES):
            dst[row0 : row0 + half, p * piece : (p + 1) * piece] = flat[p * half : (p + 1) * half]

    def receive_and_relay(t, a, src, buf):
        @pl.loop(1, n_exp)
        def _(k):
            arrival(a, k, src, buf.at[0]).wait_recv()
            relay(t, k, buf).start()

    def relays_in(t, buf):
        @pl.loop(0, n_exp)
        def _(k):
            relay(t, k, buf).wait_recv()

    receive_and_relay(0, 0, send.at[0], recv.at[0])
    unpack(recv.at[0, 0], rows, 0)
    relays_in(0, recv.at[0])
    unpack(recv.at[0, 1], rows, half)

    loads[0].wait()
    loads[1].wait()
    tile = ff // 2

    @pl.loop(0, 2)
    def _(i):
        at = pl.ds(pl.multiple_of(i * tile, tile), tile)
        gate_pre = mm(wgu[0, at], rows[...], NT)
        up_pre = mm(wgu[1, at], rows[...], NT)
        gate_dot = mm(vgu[0, at], rows[...], NT)
        up_dot = mm(vgu[1, at], rows[...], NT)
        sigma = jax.nn.sigmoid(gate_pre)
        active = gate_pre * sigma
        slope = sigma * (1.0 + gate_pre * (1.0 - sigma))
        curve = sigma * (1.0 - sigma) * (2.0 + gate_pre * (1.0 - 2.0 * sigma))
        act_dot = slope * gate_dot
        hh[at, :128] = (act_dot * up_pre + active * up_dot).astype(bf16)
        hh[at, 128:] = (active * up_pre).astype(bf16)
        keep[0, at] = up_pre * slope
        keep[1, at] = up_dot * slope + up_pre * curve * gate_dot
        keep[2, at] = active
        keep[3, at] = act_dot

    hht[...] = jnp.transpose(hh[...])
    loads[2].wait()
    loads[3].wait()
    hid_t = hht[128:]
    for p in range(PIECES):
        cols = slice(p * piece, (p + 1) * piece)
        part = mm(hid_t, wd[:, cols])
        own[0, p] = part[:half]
        xsend[0, p] = part[half:].astype(bf16)
        cross(0, p).start()
    for p in range(PIECES):
        cols = slice(p * piece, (p + 1) * piece)
        part = mm(hht[:128], wd[:, cols]) + mm(hid_t, vd[:, cols])
        own[1, p] = part[:half]
        xsend[1, p] = part[half:].astype(bf16)
        cross(1, p).start()
    for t in range(2):
        for p in range(PIECES):
            cross(t, p).wait_recv()
        total = (own[t] + xrecv[t].astype(f32)).astype(bf16).reshape(blocks, piece)
        ret_send[t] = mm(perm, total, TN).astype(bf16).reshape(n_exp, 16, piece)
        spread(1 + t, ret_send.at[t], ret_recv.at[t])

    for t in range(2):
        @pl.loop(1, n_exp)
        def _(k):
            arrival(1 + t, k, ret_send.at[t], ret_recv.at[t]).wait_recv()

        got = ret_recv[t].reshape(blocks, piece)
        his, los = [], []
        for p in range(PIECES):
            cols = slice(p * piece, (p + 1) * piece)
            both = mm(gstack[p * 256 : (p + 1) * 256], got)
            comb = both[:128] + both[128:]
            if t == 0:
                mixed[:, cols] = comb.astype(bf16)
                resid = scale * (comb - tgt[:, cols].astype(f32))
            else:
                resid = scale * comb
            hi = resid.astype(bf16)
            his.append(hi)
            los.append((resid - hi.astype(f32)).astype(bf16))
        taken = mm(btk[...], jnp.concatenate(his, axis=0)) + mm(
            btk[...], jnp.concatenate(los, axis=0)
        )
        send[1 + t] = (taken * gcol[:, :1]).astype(bf16).reshape(n_exp, 16, piece)
        spread(3 + t, send.at[1 + t], recv.at[1 + t, 0])
        relay(1 + t, 0, recv.at[1 + t]).start()

    for t in range(2):
        receive_and_relay(1 + t, 3 + t, send.at[1 + t], recv.at[1 + t])
        unpack(recv.at[1 + t, 0], cc, t * 128)
    for t in range(2):
        relays_in(1 + t, recv.at[1 + t])
        unpack(recv.at[1 + t, 1], cc, t * 128 + half)

    @pl.loop(0, 2)
    def _(i):
        at = pl.ds(pl.multiple_of(i * tile, tile), tile)
        grads = mm(wd[at], cc[...], NT)
        grad_hid = grads[:, :128]
        grad_hdot = grads[:, 128:] + mm(vd[at], cc[:128], NT)
        terms[0, at] = (grad_hdot * keep[0, at] + grad_hid * keep[1, at]).astype(bf16)
        terms[1, at] = (grad_hdot * keep[2, at] + grad_hid * keep[3, at]).astype(bf16)

    @pl.loop(1, n_exp)
    def _(k):
        for t in range(3):
            hop((0, 3, 4)[t], k, send.at[t], recv.at[t, 0]).wait_send()
        for t in range(2):
            hop(1 + t, k, ret_send.at[t], ret_recv.at[t]).wait_send()

    @pl.loop(0, n_exp)
    def _(k):
        for t in range(3):
            relay(t, k, recv.at[t]).wait_send()

    for t in range(2):
        for p in range(PIECES):
            cross(t, p).wait_send()


def out_kernel(terms, rows, hh, cc, gu, down):
    gu[0, 0] = mm(terms[0], rows[...])
    gu[0, 1] = mm(terms[1], rows[...])
    down[0] = mm(hh[...], cc[...])


def fused(n_exp, n_dp, tokens, targets, router, picks, w_gate_up, w_down, v_gate_up, v_down):
    toks, width = tokens.shape
    ff = w_down.shape[1]
    piece = width // PIECES
    half = n_exp * 4
    blocks = n_exp * 16
    onehot = picks.reshape(toks, half).astype(bf16)
    vmem = pl.BlockSpec(memory_space=pltpu.VMEM)
    hbm = pl.BlockSpec(memory_space=pl.ANY)
    dma = pltpu.SemaphoreType.DMA
    mixed, rows, hh, cc, terms = pl.pallas_call(
        functools.partial(main_kernel, n_exp, ff, width),
        out_shape=(
            jax.ShapeDtypeStruct((toks, width), bf16),
            jax.ShapeDtypeStruct((2 * half, width), bf16),
            jax.ShapeDtypeStruct((ff, 256), bf16),
            jax.ShapeDtypeStruct((4 * half, width), bf16),
            jax.ShapeDtypeStruct((2, ff, 128), bf16),
        ),
        in_specs=[vmem] * 4 + [hbm] * 4,
        out_specs=(vmem,) * 5,
        scratch_shapes=[
            pltpu.VMEM((2, ff, width), bf16),
            pltpu.VMEM((2, ff, width), bf16),
            pltpu.VMEM((ff, width), bf16),
            pltpu.VMEM((ff, width), bf16),
            pltpu.VMEM((3, n_exp, 16, piece), bf16),
            pltpu.VMEM((3, 2, n_exp, 16, piece), bf16),
            pltpu.VMEM((2, n_exp, 16, piece), bf16),
            pltpu.VMEM((2, n_exp, 16, piece), bf16),
            pltpu.VMEM((2, PIECES, half, piece), bf16),
            pltpu.VMEM((2, PIECES, half, piece), bf16),
            pltpu.VMEM((2, PIECES, half, piece), f32),
            pltpu.VMEM((256, ff), bf16),
            pltpu.VMEM((4, ff, 128), f32),
            pltpu.VMEM((PIECES * 256, blocks), bf16),
            pltpu.VMEM((blocks, PIECES * 128), bf16),
            pltpu.VMEM((blocks, 128), f32),
            dma((4,)),
            dma((5, n_exp)),
            dma((5, n_exp)),
            dma((3, n_exp)),
            dma((3, n_exp)),
            dma((2, PIECES)),
            dma((2, PIECES)),
        ],
        compiler_params=pltpu.CompilerParams(
            collective_id=0, has_side_effects=True, vmem_limit_bytes=56 * 2**20
        ),
        cost_estimate=pl.CostEstimate(
            flops=20 * 128 * ff * width, bytes_accessed=12 * ff * width, transcendentals=ff * 128
        ),
        name="experts",
    )(tokens, targets, router, onehot, w_gate_up[0], w_down[0], v_gate_up[0], v_down[0])
    tile = ff // 4
    hvp_gate_up, hvp_down = pl.pallas_call(
        out_kernel,
        grid=(4,),
        out_shape=(
            jax.ShapeDtypeStruct((1, 2, ff, width), f32),
            jax.ShapeDtypeStruct((1, ff, width), f32),
        ),
        in_specs=[
            pl.BlockSpec((2, tile, 128), lambda i: (0, i, 0)),
            pl.BlockSpec((2 * half, width), lambda i: (0, 0)),
            pl.BlockSpec((tile, 256), lambda i: (i, 0)),
            pl.BlockSpec((4 * half, width), lambda i: (0, 0)),
        ],
        out_specs=(
            pl.BlockSpec((1, 2, tile, width), lambda i: (0, 0, i, 0)),
            pl.BlockSpec((1, tile, width), lambda i: (0, i, 0)),
        ),
        compiler_params=pltpu.CompilerParams(vmem_limit_bytes=48 * 2**20),
        name="products",
    )(terms, rows, hh, cc)
    return mixed, hvp_gate_up, hvp_down


def solution(mesh):
    n_exp, n_dp = mesh.shape["expert"], mesh.shape["dp"]
    small = n_dp == 2 and n_exp <= 16
    placed = (
        P(("expert", "dp"), None),
        P(("expert", "dp"), None),
        P(),
        P(("expert", "dp"), None, None),
        P("expert", None, "dp", None),
        P("expert", "dp", None),
        P("expert", None, "dp", None),
        P("expert", "dp", None),
    )
    return jax.shard_map(
        functools.partial(fused, n_exp, n_dp) if small else local,
        mesh=mesh,
        in_specs=placed,
        out_specs=(
            P(("expert", "dp"), None),
            P("expert", None, "dp", None),
            P("expert", "dp", None),
        ),
        check_vma=False,
    )
```

```python
import functools
import math

import jax
import jax.numpy as jnp
from jax import lax
from jax.experimental import pallas as pl
from jax.experimental.pallas import tpu as pltpu
from jax.sharding import PartitionSpec as P


def regroup(block, lead):
    count, total, width = block.shape
    parted = block.reshape(count, lead, total // lead, width)
    return jnp.swapaxes(parted, 0, 1).reshape(lead, count * total // lead, width)


def local(tokens, targets, router, picks, w_gate_up, w_down, v_gate_up, v_down):
    highest = lax.Precision.HIGHEST
    n_exp = lax.axis_size("expert")
    exp_dev = w_down.shape[0]
    onehot = picks.astype(jnp.bfloat16)
    gates = jax.nn.sigmoid(jnp.dot(tokens, router, preferred_element_type=jnp.float32))
    outgoing = jnp.einsum("tec,td->ecd", onehot, tokens, preferred_element_type=jnp.float32).astype(
        jnp.bfloat16
    )
    arrived = lax.all_to_all(outgoing, "expert", split_axis=0, concat_axis=0, tiled=True)
    rows = lax.all_gather(regroup(arrived, exp_dev), "dp", axis=1, tiled=True)
    scale = 1.0 / math.sqrt(rows.shape[1])
    primal = jnp.einsum("ekfd,erd->ekfr", w_gate_up, rows, preferred_element_type=jnp.float32)
    tangent = jnp.einsum("ekfd,erd->ekfr", v_gate_up, rows, preferred_element_type=jnp.float32)
    gate_pre, up_pre = (primal[:, 0], primal[:, 1])
    gate_dot, up_dot = (tangent[:, 0], tangent[:, 1])
    sigma = jax.nn.sigmoid(gate_pre)
    active = gate_pre * sigma
    slope = sigma * (1.0 + gate_pre * (1.0 - sigma))
    curve = sigma * (1.0 - sigma) * (2.0 + gate_pre * (1.0 - 2.0 * sigma))
    act_dot = slope * gate_dot
    hidden = (active * up_pre).astype(jnp.bfloat16)
    hidden_dot = (act_dot * up_pre + active * up_dot).astype(jnp.bfloat16)
    part_out = jnp.einsum("efr,efd->erd", hidden, w_down, preferred_element_type=jnp.float32)
    part_dot = jnp.einsum(
        "efr,efd->erd", hidden_dot, w_down, preferred_element_type=jnp.float32
    ) + jnp.einsum("efr,efd->erd", hidden, v_down, preferred_element_type=jnp.float32)
    own_out, own_dot = (
        lax.psum_scatter(part_out, "dp", scatter_dimension=1, tiled=True),
        lax.psum_scatter(part_dot, "dp", scatter_dimension=1, tiled=True),
    )
    back_out = regroup(own_out.astype(jnp.bfloat16), n_exp)
    back_dot = regroup(own_dot.astype(jnp.bfloat16), n_exp)
    ret_out, ret_dot = (
        lax.all_to_all(back_out, "expert", split_axis=0, concat_axis=0, tiled=True),
        lax.all_to_all(back_dot, "expert", split_axis=0, concat_axis=0, tiled=True),
    )
    ret_out = ret_out.astype(jnp.float32)
    ret_dot = ret_dot.astype(jnp.float32)
    weighted = picks.astype(jnp.float32) * gates[:, :, None]
    combined = jnp.einsum("tec,ecd->td", weighted, ret_out, precision=highest)
    combined_dot = jnp.einsum("tec,ecd->td", weighted, ret_dot, precision=highest)
    mixed = combined.astype(jnp.bfloat16)
    resid = scale * (combined - targets.astype(jnp.float32))
    resid_dot = scale * combined_dot
    cot_send = jnp.einsum("tec,td->ecd", weighted, resid, precision=highest).astype(jnp.bfloat16)
    cdot_send = jnp.einsum("tec,td->ecd", weighted, resid_dot, precision=highest).astype(
        jnp.bfloat16
    )
    cot_got, cdot_got = (
        lax.all_to_all(cot_send, "expert", split_axis=0, concat_axis=0, tiled=True),
        lax.all_to_all(cdot_send, "expert", split_axis=0, concat_axis=0, tiled=True),
    )
    own_cot = regroup(cot_got, exp_dev)
    own_cdot = regroup(cdot_got, exp_dev)
    cot_rows, cdot_rows = (
        lax.all_gather(own_cot, "dp", axis=1, tiled=True),
        lax.all_gather(own_cdot, "dp", axis=1, tiled=True),
    )
    grad_hid = jnp.einsum("erd,efd->efr", cot_rows, w_down, preferred_element_type=jnp.float32)
    grad_hdot = jnp.einsum(
        "erd,efd->efr", cdot_rows, w_down, preferred_element_type=jnp.float32
    ) + jnp.einsum("erd,efd->efr", cot_rows, v_down, preferred_element_type=jnp.float32)
    hvp_down = jnp.einsum(
        "efr,erd->efd", hidden_dot, cot_rows, preferred_element_type=jnp.float32
    ) + jnp.einsum("efr,erd->efd", hidden, cdot_rows, preferred_element_type=jnp.float32)
    gate_term = (
        (grad_hdot * up_pre + grad_hid * up_dot) * slope + grad_hid * up_pre * curve * gate_dot
    ).astype(jnp.bfloat16)
    up_term = (grad_hdot * active + grad_hid * act_dot).astype(jnp.bfloat16)
    both_terms = jnp.stack([gate_term, up_term], axis=1)
    hvp_gate_up = jnp.einsum("ekfr,erd->ekfd", both_terms, rows, preferred_element_type=jnp.float32)
    return (mixed, hvp_gate_up, hvp_down)


f32, bf16 = jnp.float32, jnp.bfloat16
NT = (((1,), (1,)), ((), ()))
TN = (((0,), (0,)), ((), ()))
ORDER = (2, 3, 1, 0)
PIECES = 4


def mm(a, b, dims=(((1,), (0,)), ((), ()))):
    return lax.dot_general(a, b, dims, preferred_element_type=f32)


def iota2(shape, dim):
    return lax.broadcasted_iota(jnp.int32, shape, dim)


def main_kernel(
    n_exp, ff, width,
    tok, tgt, router, picks, wgu_hbm, wd_hbm, vgu_hbm, vd_hbm,
    mixed_out, rows_out, hh_out, cc_out, terms_out,
    wgu, vgu, wd, vd,
    send, recv, ret_send, ret_recv, xsend, xrecv, own, hht, keep, gstack, btk, gcol,
    mixed, rows, hh, cc, terms, chosen,
    wsem, osem, ssem, rsem, fs_sem, fr_sem, xs_sem, xr_sem,
):
    me = lax.axis_index("expert")
    peer = 1 - lax.axis_index("dp")
    piece = width // PIECES
    half = n_exp * 4
    blocks = n_exp * 16
    scale = 1.0 / math.sqrt(2 * half)

    loads = [
        pltpu.make_async_copy(src, dst, wsem.at[i])
        for i, (src, dst) in enumerate(
            [(wgu_hbm, wgu), (vgu_hbm, vgu), (wd_hbm, wd), (vd_hbm, vd)]
        )
    ]
    for load in loads:
        load.start()

    barrier = pltpu.get_barrier_semaphore()

    @pl.loop(1, n_exp)
    def _(k):
        pl.semaphore_signal(
            barrier, inc=1, device_id={"expert": lax.rem(me + k, n_exp)},
            device_id_type=pl.DeviceIdType.MESH,
        )

    pl.semaphore_signal(barrier, inc=1, device_id={"dp": peer}, device_id_type=pl.DeviceIdType.MESH)

    z, lane = lax.div(me, 4), lax.rem(me, 4)

    def group(s):
        if s == 0:
            return z
        if s == 1:
            return z + 1 - 2 * lax.rem(z, 2)
        if s == 2:
            return lax.rem(z + 2, 4)
        return 3 - z

    def remote(src, dst, send_sem, recv_sem, **axis):
        return pltpu.make_async_remote_copy(
            src_ref=src, dst_ref=dst, send_sem=send_sem, recv_sem=recv_sem,
            device_id=axis, device_id_type=pl.DeviceIdType.MESH,
        )

    def four(s):
        return pl.ds(group(s) * 4, 4)

    def spread(t, s, src, dst):
        if s == 0:
            dst[me] = src[me]

        @pl.loop(1 if s == 0 else 0, 4)
        def _(j):
            to = group(s) * 4 + lax.rem(lane + j, 4)
            at = (t, 3 + j) if s == 0 else (t, s)
            remote(src.at[to], dst.at[me], ssem.at[at], rsem.at[at], expert=to).start()

    def arrived(t, s, dst):
        if s == 0:
            for j in range(1, 4):
                come = z * 4 + lax.rem(lane + 4 - j, 4)
                ref = dst.at[come]
                remote(ref, ref, ssem.at[t, 3 + j], rsem.at[t, 3 + j], expert=come).wait_recv()
        else:
            ref = dst.at[four(s)]
            remote(ref, ref, ssem.at[t, s], rsem.at[t, s], expert=group(s) * 4).wait_recv()

    def sent(t, src):
        for j in range(1, 4):
            to = z * 4 + lax.rem(lane + j, 4)
            ref = src.at[to]
            remote(ref, ref, ssem.at[t, 3 + j], rsem.at[t, 3 + j], expert=to).wait_send()
        for s in range(1, 4):
            ref = src.at[four(s)]
            remote(ref, ref, ssem.at[t, s], rsem.at[t, s], expert=group(s) * 4).wait_send()

    def relay(t, s):
        return remote(
            recv.at[t, 0, four(s)], recv.at[t, 1, four(s)], fs_sem.at[t, s], fr_sem.at[t, s], dp=peer
        )

    def cross(t, s):
        g = group(s)
        return remote(xsend.at[t, g], xrecv.at[t, g], xs_sem.at[t, s], xr_sem.at[t, s], dp=peer)

    def write(i, src, dst):
        copy = pltpu.make_async_copy(src, dst, osem.at[i])
        copy.start()
        return copy

    row_b, col_b = iota2((blocks, half), 0), iota2((blocks, half), 1)
    all_pieces = jnp.where(
        ((row_b >> 4) == (col_b >> 2)) & ((row_b & 3) == (col_b & 3)), 1.0, 0.0
    ).astype(bf16)
    for e in range(n_exp):
        chosen[e * 4 : e * 4 + 4] = picks[e].astype(f32)
    picked_t = mm(all_pieces, chosen[...].astype(bf16))
    row_t = iota2(picked_t.shape, 0)
    for p in range(PIECES):
        btk[:, p * 128 : (p + 1) * 128] = jnp.where(
            ((row_t >> 2) & 3) == p, picked_t, 0.0
        ).astype(bf16)
    stacked = jnp.concatenate([tok[:, p * piece : (p + 1) * piece] for p in range(PIECES)], axis=0)
    send[0] = mm(btk[...], stacked).astype(bf16).reshape(n_exp, 16, piece)
    pl.semaphore_wait(barrier, n_exp)
    for s in ORDER:
        spread(0, s, send.at[0], recv.at[0, 0])

    gates = jax.nn.sigmoid(mm(tok[...], router[...], NT))
    g_hi = gates.astype(bf16)
    g_lo = (gates - g_hi.astype(f32)).astype(bf16)
    lane_e, col_e = iota2((n_exp, blocks), 0), iota2((n_exp, blocks), 1)
    widen = jnp.where(lane_e == (col_e >> 4), 1.0, 0.0).astype(bf16)
    weight = jnp.transpose(picked_t) * (mm(g_hi, widen) + mm(g_lo, widen))
    w_hi = weight.astype(bf16).astype(f32)
    w_lo = weight - w_hi
    col_w = iota2(weight.shape, 1)
    for p in range(PIECES):
        at_piece = ((col_w >> 2) & 3) == p
        gstack[p * 256 : p * 256 + 128] = jnp.where(at_piece, w_hi, 0.0).astype(bf16)
        gstack[p * 256 + 128 : p * 256 + 256] = jnp.where(at_piece, w_lo, 0.0).astype(bf16)
    by_expert = mm(picked_t.astype(bf16), g_hi) + mm(picked_t.astype(bf16), g_lo)
    own_lane = (iota2(by_expert.shape, 0) >> 4) == iota2(by_expert.shape, 1)
    gcol[...] = jnp.broadcast_to(
        jnp.sum(jnp.where(own_lane, by_expert, 0.0), axis=1, keepdims=True), gcol.shape
    )


    def to_rows_matrix():
        rr, cp = iota2((blocks, blocks), 0), iota2((blocks, blocks), 1)
        inside = lax.rem(rr, half)
        want = (inside >> 2) * 16 + lax.div(rr, half) * 4 + (inside & 3)
        return jnp.where(cp == want, 1.0, 0.0).astype(bf16)

    perm = to_rows_matrix()

    def unpack(buf, dst, row0):
        flat = mm(perm, buf[...].reshape(blocks, piece)).astype(bf16)
        for p in range(PIECES):
            dst[row0 : row0 + half, p * piece : (p + 1) * piece] = flat[p * half : (p + 1) * half]

    def relay_in(t, a, s):
        arrived(a, s, recv.at[t, 0])
        relay(t, s).start()

    for s in ORDER:
        relay_in(0, 0, s)
    unpack(recv.at[0, 0], rows, 0)
    for s in ORDER:
        relay(0, s).wait_recv()
    unpack(recv.at[0, 1], rows, half)
    writes = [write(0, rows, rows_out)]

    loads[0].wait()
    loads[1].wait()
    tile = ff // 2

    @pl.loop(0, 2)
    def _(i):
        at = pl.ds(pl.multiple_of(i * tile, tile), tile)
        gate_pre = mm(wgu[0, at], rows[...], NT)
        up_pre = mm(wgu[1, at], rows[...], NT)
        gate_dot = mm(vgu[0, at], rows[...], NT)
        up_dot = mm(vgu[1, at], rows[...], NT)
        sigma = jax.nn.sigmoid(gate_pre)
        active = gate_pre * sigma
        slope = sigma * (1.0 + gate_pre * (1.0 - sigma))
        curve = sigma * (1.0 - sigma) * (2.0 + gate_pre * (1.0 - 2.0 * sigma))
        act_dot = slope * gate_dot
        hh[at, :128] = (act_dot * up_pre + active * up_dot).astype(bf16)
        hh[at, 128:] = (active * up_pre).astype(bf16)
        keep[0, at] = up_pre * slope
        keep[1, at] = up_dot * slope + up_pre * curve * gate_dot
        keep[2, at] = active
        keep[3, at] = act_dot

    writes.append(write(1, hh, hh_out))
    hht[...] = jnp.transpose(hh[...])
    loads[2].wait()
    loads[3].wait()
    hid_t = hht[128:]
    for t in range(2):
        for p in range(PIECES):
            cols = slice(p * piece, (p + 1) * piece)
            if t == 0:
                part = mm(hid_t, wd[:, cols])
            else:
                part = mm(hht[:128], wd[:, cols]) + mm(hid_t, vd[:, cols])
            for g in range(4):
                own[t, g, p] = part[g * 16 : g * 16 + 16]
                xsend[t, g, p] = part[half + g * 16 : half + g * 16 + 16].astype(bf16)
        for s in ORDER:
            cross(t, s).start()

    rq, cq = iota2((64, 64), 0), iota2((64, 64), 1)
    perm_group = jnp.where(
        cq == ((rq >> 2) & 3) * 16 + (rq >> 4) * 4 + (rq & 3), 1.0, 0.0
    ).astype(bf16)

    def give_back(t, s):
        g = group(s)
        cross(t, s).wait_recv()
        total = (own[t, g] + xrecv[t, g].astype(f32)).astype(bf16).reshape(64, piece)
        ret_send[t, four(s)] = mm(perm_group, total).astype(bf16).reshape(4, 16, piece)
        spread(1 + t, s, ret_send.at[t], ret_recv.at[t])

    def combine(t):
        for s in ORDER:
            arrived(1 + t, s, ret_recv.at[t])
        got = ret_recv[t].reshape(blocks, piece)
        his, los = [], []
        for p in range(PIECES):
            cols = slice(p * piece, (p + 1) * piece)
            both = mm(gstack[p * 256 : (p + 1) * 256], got)
            comb = both[:128] + both[128:]
            if t == 0:
                mixed[:, cols] = comb.astype(bf16)
                resid = scale * (comb - tgt[:, cols].astype(f32))
            else:
                resid = scale * comb
            hi = resid.astype(bf16)
            his.append(hi)
            los.append((resid - hi.astype(f32)).astype(bf16))
        taken = mm(btk[...], jnp.concatenate(his, axis=0)) + mm(
            btk[...], jnp.concatenate(los, axis=0)
        )
        send[1 + t] = (taken * gcol[:, :1]).astype(bf16).reshape(n_exp, 16, piece)
        for s in ORDER:
            spread(3 + t, s, send.at[1 + t], recv.at[1 + t, 0])

    for s in ORDER:
        give_back(0, s)
    for s in ORDER[:2]:
        give_back(1, s)
    combine(0)
    writes.append(write(2, mixed, mixed_out))
    for s in ORDER[2:]:
        give_back(1, s)
    for s in ORDER[:2]:
        relay_in(1, 3, s)
    combine(1)
    for s in ORDER[2:]:
        relay_in(1, 3, s)
    unpack(recv.at[1, 0], cc, 0)
    for s in ORDER:
        relay(1, s).wait_recv()
    unpack(recv.at[1, 1], cc, half)

    tile = ff // 4
    for i, s in enumerate(ORDER):
        at = slice(i * tile, (i + 1) * tile)
        grad_hid = mm(wd[at], cc[:128], NT)
        grad_v = mm(vd[at], cc[:128], NT)
        keep[1, at] = grad_hid * keep[1, at] + grad_v * keep[0, at]
        keep[3, at] = grad_hid * keep[3, at] + grad_v * keep[2, at]
        relay_in(2, 4, s)
    unpack(recv.at[2, 0], cc, 128)
    for s in ORDER:
        relay(2, s).wait_recv()
    unpack(recv.at[2, 1], cc, 128 + half)
    writes.append(write(3, cc, cc_out))
    for i in range(4):
        at = slice(i * tile, (i + 1) * tile)
        grad_c = mm(wd[at], cc[128:], NT)
        terms[0, at] = (grad_c * keep[0, at] + keep[1, at]).astype(bf16)
        terms[1, at] = (grad_c * keep[2, at] + keep[3, at]).astype(bf16)
    writes.append(write(4, terms, terms_out))

    for t in range(3):
        sent((0, 3, 4)[t], send.at[t])
        for s in ORDER:
            relay(t, s).wait_send()
    for t in range(2):
        sent(1 + t, ret_send.at[t])
        for s in ORDER:
            cross(t, s).wait_send()
    for copy in writes:
        copy.wait()


def out_kernel(terms, rows, hh, cc, mixed, gu, down, mixed_out):
    mixed_out[...] = mixed[...]
    gu[0, 0] = mm(terms[0], rows[...])
    gu[0, 1] = mm(terms[1], rows[...])
    down[0] = mm(hh[...], cc[...])


def fused(n_exp, n_dp, tokens, targets, router, picks, w_gate_up, w_down, v_gate_up, v_down):
    toks, width = tokens.shape
    ff = w_down.shape[1]
    piece = width // PIECES
    half = n_exp * 4
    blocks = n_exp * 16
    vmem = pl.BlockSpec(memory_space=pltpu.VMEM)
    hbm = pl.BlockSpec(memory_space=pl.ANY)
    dma = pltpu.SemaphoreType.DMA
    mixed, rows, hh, cc, terms = pl.pallas_call(
        functools.partial(main_kernel, n_exp, ff, width),
        out_shape=(
            jax.ShapeDtypeStruct((toks, width), bf16),
            jax.ShapeDtypeStruct((2 * half, width), bf16),
            jax.ShapeDtypeStruct((ff, 256), bf16),
            jax.ShapeDtypeStruct((4 * half, width), bf16),
            jax.ShapeDtypeStruct((2, ff, 128), bf16),
        ),
        in_specs=[vmem] * 4 + [hbm] * 4,
        out_specs=(hbm,) * 5,
        scratch_shapes=[
            pltpu.VMEM((2, ff, width), bf16),
            pltpu.VMEM((2, ff, width), bf16),
            pltpu.VMEM((ff, width), bf16),
            pltpu.VMEM((ff, width), bf16),
            pltpu.VMEM((3, n_exp, 16, piece), bf16),
            pltpu.VMEM((3, 2, n_exp, 16, piece), bf16),
            pltpu.VMEM((2, n_exp, 16, piece), bf16),
            pltpu.VMEM((2, n_exp, 16, piece), bf16),
            pltpu.VMEM((2, 4, PIECES, 16, piece), bf16),
            pltpu.VMEM((2, 4, PIECES, 16, piece), bf16),
            pltpu.VMEM((2, 4, PIECES, 16, piece), f32),
            pltpu.VMEM((256, ff), bf16),
            pltpu.VMEM((4, ff, 128), f32),
            pltpu.VMEM((PIECES * 256, blocks), bf16),
            pltpu.VMEM((blocks, PIECES * 128), bf16),
            pltpu.VMEM((blocks, 128), f32),
            pltpu.VMEM((toks, width), bf16),
            pltpu.VMEM((2 * half, width), bf16),
            pltpu.VMEM((ff, 256), bf16),
            pltpu.VMEM((4 * half, width), bf16),
            pltpu.VMEM((2, ff, 128), bf16),
            pltpu.VMEM((half, toks), f32),
            dma((4,)),
            dma((5,)),
            dma((5, 7)),
            dma((5, 7)),
            dma((3, 4)),
            dma((3, 4)),
            dma((2, 4)),
            dma((2, 4)),
        ],
        compiler_params=pltpu.CompilerParams(
            collective_id=0, has_side_effects=True, vmem_limit_bytes=56 * 2**20
        ),
        cost_estimate=pl.CostEstimate(
            flops=20 * 128 * ff * width, bytes_accessed=12 * ff * width, transcendentals=ff * 128
        ),
        name="experts",
    )(tokens, targets, router.T, jnp.transpose(picks, (1, 2, 0)), w_gate_up[0], w_down[0], v_gate_up[0], v_down[0])
    tile = ff // 4
    hvp_gate_up, hvp_down, mixed = pl.pallas_call(
        out_kernel,
        grid=(4,),
        out_shape=(
            jax.ShapeDtypeStruct((1, 2, ff, width), f32),
            jax.ShapeDtypeStruct((1, ff, width), f32),
            jax.ShapeDtypeStruct((toks, width), bf16),
        ),
        in_specs=[
            pl.BlockSpec((2, tile, 128), lambda i: (0, i, 0)),
            pl.BlockSpec((2 * half, width), lambda i: (0, 0)),
            pl.BlockSpec((tile, 256), lambda i: (i, 0)),
            pl.BlockSpec((4 * half, width), lambda i: (0, 0)),
            pl.BlockSpec((toks // 4, width), lambda i: (i, 0)),
        ],
        out_specs=(
            pl.BlockSpec((1, 2, tile, width), lambda i: (0, 0, i, 0)),
            pl.BlockSpec((1, tile, width), lambda i: (0, i, 0)),
            pl.BlockSpec((toks // 4, width), lambda i: (i, 0)),
        ),
        compiler_params=pltpu.CompilerParams(vmem_limit_bytes=60 * 2**20),
        name="products",
    )(terms, rows, hh, cc, mixed)
    return mixed, hvp_gate_up, hvp_down


def solution(mesh):
    n_exp, n_dp = mesh.shape["expert"], mesh.shape["dp"]
    small = n_dp == 2 and n_exp == 16
    placed = (
        P(("expert", "dp"), None),
        P(("expert", "dp"), None),
        P(),
        P(("expert", "dp"), None, None),
        P("expert", None, "dp", None),
        P("expert", "dp", None),
        P("expert", None, "dp", None),
        P("expert", "dp", None),
    )
    return jax.shard_map(
        functools.partial(fused, n_exp, n_dp) if small else local,
        mesh=mesh,
        in_specs=placed,
        out_specs=(
            P(("expert", "dp"), None),
            P("expert", None, "dp", None),
            P("expert", "dp", None),
        ),
        check_vma=False,
    )
```
